768 devices in a mesh: mem: 32 (over y, x), patch: 24 (over z, core).
Axes of the slice: x: 4, y: 8, z: 12, core: 2. Of those that a mesh axis runs over, the one named last changes fastest.
Arguments:
- state: bfloat16 [1024, 393216], P('mem', 'patch'), may hold values from -6 to 6
- obs_ens: bfloat16 [1024, 196608], P('mem', 'patch'), may hold values from -6 to 6
- obs_values: float32 [196608], P('patch'), may hold values from -8 to 8
- obs_weight: float32 [196608], P('patch'), may hold values from 0.2 to 5
- counts: int32 [768], P('patch'), may hold values from 32 to 256
Outputs:
- analysis: bfloat16 [1024, 393216], P('mem', 'patch')
The draws below stay inside these ranges and needn't reach their ends.
Inputs may be any that keep to these rules, and one draw needn't show every extreme that they name: Region r uses the first counts[r] of its 256 observations.
All inputs are finite; a program needn't handle non-finite values. Where the reference program divides by a largest or mean magnitude, that divisor is 1e-20 or more.
Results may differ from the reference program's by a relative error of at most 0.0047.
Values may be sent and summed in bfloat16 or wider, within the bound.
No kernel may reach another device: no remote copies, remote signals or barrier semaphores. Data moves between devices by JAX's collectives and lax.ppermute only.
A program may use at most 32 MiB of HBM per device.

```python
import math
import jax
import jax.numpy as jnp
from jax import lax

MEMBERS = 1024
REGION_ROWS = 512
OBS_OWN = 256
DEGREE = 7
REGIONS_PATCH = 32
REGIONS = 768
NROWS = 393216
NOBS = 196608


def set_ends(array, stream_key, low, high):
    longest = array.shape.index(max(array.shape))
    spots = []
    for shift in (0, 1):
        where = [jax.random.randint(jax.random.fold_in(stream_key, axis), (), 0, length) for axis, length in enumerate(array.shape)]
        where[longest] = (where[longest] + shift) % array.shape[longest]
        spots.append(tuple(where))
    return array.at[spots[0]].set(low).at[spots[1]].set(high)


def level_of(key, extent, cuts, least, top_value):
    loudness = 1.0
    for axis_at, blocks in cuts:
        heights = jax.random.uniform(jax.random.fold_in(jax.random.fold_in(key, 6), axis_at), (blocks,), jnp.float32, least / len(cuts), top_value / len(cuts))
        loudness = loudness * jnp.repeat(jnp.exp(heights), extent[axis_at] // blocks).reshape((-1,) + (1,) * (len(extent) - 1 - axis_at))
    return loudness


def bell_draw(own_key, dims, width, reach, shards=(), kind=jnp.bfloat16):
    array = jax.random.normal(own_key, dims, jnp.float32) * width
    if len(shards) > 0:
        array = level_of(own_key, dims, shards, -0.22, 0.18) * array
    return jnp.clip(array, min=-reach, max=reach).astype(kind)


def setup_inputs(seed: int = 0) -> dict:
    arg_keys = jax.random.split(jax.random.key(seed), 6)
    return {
        "state": bell_draw(arg_keys[0], (MEMBERS, NROWS), 1.0, 6.0, ((0, 32), (1, 24))),
        "obs_ens": bell_draw(arg_keys[1], (MEMBERS, NOBS), 1.0, 6.0, ((0, 32), (1, 24))),
        "obs_values": bell_draw(arg_keys[2], (NOBS,), 1.5, 8.0, ((0, 24),), jnp.float32),
        "obs_weight": jnp.clip(jnp.exp(math.log(5.0) - 3.218876 * jax.random.uniform(arg_keys[3], (NOBS,), jnp.float32) ** level_of(arg_keys[3], (NOBS,), ((0, 24),), -0.2, 0.2)), 0.2, 5.0),
        "counts": set_ends(jax.random.randint(arg_keys[4], (REGIONS,), OBS_OWN // 8, OBS_OWN + 1), jax.random.fold_in(arg_keys[4], 1), OBS_OWN // 8, OBS_OWN).astype(jnp.int32),
    }


def root_curve(values):
    lifted = jnp.sqrt(1.0 + values)
    return -1.0 / (lifted * (1.0 + lifted))

def inverse_curve(values):
    return 1.0 / (1.0 + values)

def chebyshev(upper, curve):
    number = DEGREE + 1
    theta = (jnp.arange(number, dtype=jnp.float32) + 0.5) * (math.pi / number)
    nodes = upper * (jnp.cos(theta) + 1.0) * 0.5
    samples = curve(nodes)
    orders = jnp.arange(number, dtype=jnp.float32)
    table = jnp.cos(orders[:, None] * theta[None, :])
    coefs = 2.0 / number * lax.optimization_barrier(jnp.sum(table * samples[None, :], axis=1))
    return coefs * jnp.where(orders == 0.0, 0.5, 1.0)

def clenshaw(block, matrix, coefs):
    nearer = coefs[DEGREE] * block
    farther = jnp.zeros_like(block)
    for order in range(DEGREE - 1, 0, -1):
        current = coefs[order] * block + 2.0 * jnp.dot(nearer, matrix, precision=lax.Precision.HIGHEST) - farther
        farther, nearer = (nearer, current)
    return coefs[0] * block + jnp.dot(nearer, matrix, precision=lax.Precision.HIGHEST) - farther

def perturb_obs(obs_block, values, weights, count):
    full = obs_block.astype(jnp.float32)
    centre = lax.optimization_barrier(jnp.mean(full, axis=0))
    mask = (jnp.arange(values.shape[0], dtype=jnp.int32) < count).astype(jnp.float32)
    root = jnp.sqrt(weights * mask)
    gains = ((full - centre[None, :]) * root[None, :]).astype(jnp.bfloat16)
    innov = (root * (values - centre)).astype(jnp.bfloat16)
    return jnp.concatenate([gains, innov[None, :]], axis=0)

def transform(region_state, stacked):
    gains = stacked[:-1]
    innov = stacked[-1].astype(jnp.float32)
    members = gains.shape[0]
    normal = jnp.dot(gains.T, gains, preferred_element_type=jnp.float32) / (members - 1)
    upper = jnp.max(lax.optimization_barrier(jnp.sum(jnp.abs(normal), axis=1))) + 1e-06
    shifted = normal * (2.0 / upper) - jnp.eye(normal.shape[0], dtype=jnp.float32)
    full = region_state.astype(jnp.float32)
    centre = lax.optimization_barrier(jnp.mean(full, axis=0))
    spread = (full - centre[None, :]).astype(jnp.bfloat16)
    product = jnp.dot(spread.T, gains, preferred_element_type=jnp.float32)
    mixed = clenshaw(product, shifted, chebyshev(upper, root_curve)).astype(jnp.bfloat16)
    mean_weights = clenshaw(innov[None, :], shifted, chebyshev(upper, inverse_curve))[0]
    mean_shift = jnp.dot(product, mean_weights, precision=lax.Precision.HIGHEST) / (members - 1)
    update = jnp.dot(gains, mixed.T, preferred_element_type=jnp.float32) / (members - 1)
    return (full + mean_shift[None, :] + update).astype(jnp.bfloat16)

def reference(state, obs_ens, obs_values, obs_weight, counts):
    order = jnp.arange(REGIONS, dtype=jnp.int32)

    def own_part(region):
        start = region * OBS_OWN
        block = lax.dynamic_slice_in_dim(obs_ens, start, OBS_OWN, 1)
        values = lax.dynamic_slice_in_dim(obs_values, start, OBS_OWN, 0)
        weights = lax.dynamic_slice_in_dim(obs_weight, start, OBS_OWN, 0)
        return perturb_obs(block, values, weights, counts[region])
    stacked = lax.map(own_part, order)
    half = OBS_OWN // 2

    def one_region(region):
        left = stacked[(region - REGIONS_PATCH) % REGIONS][:, OBS_OWN - half:]
        right = stacked[(region + REGIONS_PATCH) % REGIONS][:, :half]
        joined = jnp.concatenate([left, stacked[region], right], axis=1)
        block = lax.dynamic_slice_in_dim(state, region * REGION_ROWS, REGION_ROWS, 1)
        return transform(block, joined)
    result = lax.map(one_region, order)
    return jnp.transpose(result, (1, 0, 2)).reshape(MEMBERS, NROWS)
```

```python
import math

import jax
import jax.numpy as jnp
import numpy as np
from jax import lax
from jax.experimental import pallas as pl
from jax.experimental.pallas import tpu as pltpu
from jax.sharding import PartitionSpec as P

DEGREE = 7
NODES = DEGREE + 1
PAD = 16
LIMIT = 30 * 1024 * 1024


def tables():
    theta = (np.arange(NODES) + 0.5) * (math.pi / NODES)
    orders = np.arange(NODES)
    table = np.zeros((2 * NODES, 128), np.float32)
    weight = np.where(orders == 0, 0.5, 1.0) * 2.0 / NODES
    table[:NODES, :NODES] = np.cos(orders[:, None] * theta[None, :]) * weight[:, None]
    table[NODES, :NODES] = (np.cos(theta) + 1.0) * 0.5
    return table


def dot(left, right):
    return jnp.dot(left, right, preferred_element_type=jnp.float32)


def split(x):
    high = x.astype(jnp.bfloat16)
    return high, (x - high.astype(jnp.float32)).astype(jnp.bfloat16)


def product(left, right):
    return dot(left[0], right[0]) + (dot(left[0], right[1]) + dot(left[1], right[0]))


def gains_kernel(obs_ref, side_ref, head_ref, tail_ref):
    members, own = obs_ref.shape
    half = own // 2
    for part, out in ((0, head_ref), (1, tail_ref)):
        columns = slice(part * half, (part + 1) * half)
        full = obs_ref[:, columns].astype(jnp.float32)
        centre = jnp.sum(full, axis=0, keepdims=True) * (1.0 / members)
        root = side_ref[0:1, columns]
        out[0:members, :] = ((full - centre) * root).astype(jnp.bfloat16)
        innov = root * (side_ref[1:2, columns] - centre)
        out[members:, :] = jnp.broadcast_to(innov, (PAD, half)).astype(jnp.bfloat16)


def weights_kernel(left_ref, head_ref, tail_ref, right_ref, table_ref, out_ref, gains, turned):
    members, sites = gains.shape
    half = sites // 4
    parts = (left_ref, head_ref, tail_ref, right_ref)
    for part, ref in enumerate(parts):
        block = ref[0:members, :]
        gains[:, part * half : (part + 1) * half] = block
        turned[part * half : (part + 1) * half, :] = block.T
    innov = jnp.concatenate([ref[members:, :] for ref in parts], axis=1)

    normal = dot(turned[...], gains[...]) * (1.0 / (members - 1))
    upper = jnp.max(jnp.sum(jnp.abs(normal), axis=0, keepdims=True), axis=1, keepdims=True) + 1e-06
    nodes = upper * table_ref[NODES : NODES + 1, :]
    lifted = jnp.sqrt(1.0 + nodes)
    table = table_ref[0:NODES, :]
    roots = jnp.sum(table * (-1.0 / (lifted * (1.0 + lifted))), axis=1, keepdims=True)
    inverses = jnp.sum(table * (1.0 / (1.0 + nodes)), axis=1, keepdims=True)
    a = [roots[k : k + 1, :] for k in range(NODES)]
    e = [inverses[k : k + 1, :] for k in range(NODES)]

    rows = lax.broadcasted_iota(jnp.int32, normal.shape, 0)
    columns = lax.broadcasted_iota(jnp.int32, normal.shape, 1)
    eye = jnp.where(rows == columns, 1.0, 0.0).astype(jnp.float32)
    scaled = normal * (2.0 / upper)
    scaled_parts = split(scaled)
    t1 = scaled - eye
    t2 = 2.0 * product(scaled_parts, scaled_parts) - 4.0 * scaled + eye
    t2_parts = split(t2)
    t3 = 2.0 * (product(t2_parts, scaled_parts) - t2) - t1
    t4 = 2.0 * product(t2_parts, t2_parts) - eye
    t4_parts = split(t4)

    def polynomial(c):
        inner = c[5] * t1 + c[6] * t2 + c[7] * t3
        outer = c[0] * eye + (c[1] - c[7]) * t1 + (c[2] - c[6]) * t2 + (c[3] - c[5]) * t3 + c[4] * t4
        return outer + 2.0 * product(split(inner), t4_parts)

    root = split(polynomial(a))
    inverse = split(polynomial(e))
    mean_weights = dot(innov, inverse[0]) + dot(innov, inverse[1])
    shift = split(mean_weights * (1.0 / (members - 1)))
    turned_now = turned[...]
    rows_shift = dot(shift[0], turned_now) + dot(shift[1], turned_now)
    high, low = split(rows_shift)
    out_ref[members:, :] = jnp.concatenate([high[: PAD // 2], low[: PAD // 2]], axis=0)
    reduced = (dot(root[0], turned_now) + dot(root[1], turned_now)).astype(jnp.bfloat16)
    out_ref[0:members, :] = (dot(gains[...], reduced) * (1.0 / (members - 1))).astype(jnp.bfloat16)


def apply_kernel(state_ref, weights_ref, out_ref, spread):
    members = state_ref.shape[0]
    total = jnp.sum(state_ref[...].astype(jnp.float32), axis=0, keepdims=True)
    centre = total * (1.0 / members)
    spread[...] = (state_ref[...].astype(jnp.float32) - centre).astype(jnp.bfloat16)
    shifts = dot(weights_ref[members:, :], spread[...])
    shift = shifts[0:1, :] + shifts[PAD // 2 : PAD // 2 + 1, :]
    step = 256
    for start in range(0, members, step):
        block = slice(start, start + step)
        update = dot(weights_ref[block, :], spread[...])
        out_ref[block, :] = (state_ref[block, :].astype(jnp.float32) + shift + update).astype(jnp.bfloat16)


def call(kernel, out_shape, scratch, flops, nbytes, *args):
    return pl.pallas_call(
        kernel,
        out_shape=out_shape,
        in_specs=[pl.BlockSpec(memory_space=pltpu.VMEM)] * len(args),
        out_specs=jax.tree.map(lambda _: pl.BlockSpec(memory_space=pltpu.VMEM), out_shape),
        scratch_shapes=scratch,
        compiler_params=pltpu.CompilerParams(vmem_limit_bytes=LIMIT),
        cost_estimate=pl.CostEstimate(flops=flops, bytes_accessed=nbytes, transcendentals=0),
    )(*args)


def on_device(state, obs_ens, obs_values, obs_weight, counts):
    mem_index = lax.axis_index("mem")
    own = obs_ens.shape[1] // lax.axis_size("mem")
    half = own // 2
    patches = lax.axis_size("patch")
    region_obs = lax.all_to_all(obs_ens, "mem", split_axis=1, concat_axis=0, tiled=True)
    region_state = lax.all_to_all(state, "mem", split_axis=1, concat_axis=0, tiled=True)
    members, columns = region_state.shape

    values = lax.dynamic_slice_in_dim(obs_values, mem_index * own, own, 0)
    weights = lax.dynamic_slice_in_dim(obs_weight, mem_index * own, own, 0)
    count = lax.dynamic_slice_in_dim(counts, mem_index, 1, 0)[0]
    mask = (jnp.arange(own, dtype=jnp.int32) < count).astype(jnp.float32)
    side = jnp.stack([jnp.sqrt(weights * mask), values])

    edge = jax.ShapeDtypeStruct((members + PAD, half), jnp.bfloat16)
    head, tail = call(gains_kernel, (edge, edge), [], 10**6, 2 * 10**6, region_obs, side)
    left = lax.ppermute(tail, "patch", [(i, (i + 1) % patches) for i in range(patches)])
    right = lax.ppermute(head, "patch", [((i + 1) % patches, i) for i in range(patches)])
    sites = 2 * own
    transform = call(
        weights_kernel,
        jax.ShapeDtypeStruct((members + PAD, members), jnp.bfloat16),
        [pltpu.VMEM((members, sites), jnp.bfloat16), pltpu.VMEM((sites, members), jnp.bfloat16)],
        7 * 10**9, 4 * 10**6,
        left, head, tail, right, jnp.asarray(tables()),
    )
    analysed = call(
        apply_kernel,
        jax.ShapeDtypeStruct((members, columns), jnp.bfloat16),
        [pltpu.VMEM((members, columns), jnp.bfloat16)],
        2 * 10**9, 4 * 10**6,
        region_state, transform,
    )
    return lax.all_to_all(analysed, "mem", split_axis=0, concat_axis=1, tiled=True)


def solution(mesh):
    placed = (P("mem", "patch"), P("mem", "patch"), P("patch"), P("patch"), P("patch"))
    return jax.shard_map(
        on_device, mesh=mesh, in_specs=placed, out_specs=P("mem", "patch"), check_vma=False
    )
```

```python
import math

import jax
import jax.numpy as jnp
import numpy as np
from jax import lax
from jax.experimental import pallas as pl
from jax.experimental.pallas import tpu as pltpu
from jax.sharding import PartitionSpec as P

DEGREE = 7
NODES = DEGREE + 1
PAD = 16
HIGH, LOW, ONES = 0, 1, 2


def tables():
    theta = (np.arange(NODES) + 0.5) * (math.pi / NODES)
    orders = np.arange(NODES)
    table = np.zeros((2 * NODES, 128), np.float32)
    weight = np.where(orders == 0, 0.5, 1.0) * 2.0 / NODES
    table[:NODES, :NODES] = np.cos(orders[:, None] * theta[None, :]) * weight[:, None]
    table[NODES, :NODES] = (np.cos(theta) + 1.0) * 0.5
    return table


def dot(left, right):
    return jnp.dot(left, right, preferred_element_type=jnp.float32)


def split(x):
    high = x.astype(jnp.bfloat16)
    return high, (x - high.astype(jnp.float32)).astype(jnp.bfloat16)


def product(left, right):
    return dot(left[0], right[0]) + (dot(left[0], right[1]) + dot(left[1], right[0]))


def gains_kernel(place_ref, obs_ref, values_ref, weights_ref, counts_ref, head_ref, tail_ref):
    members, own = obs_ref.shape
    half = own // 2
    region = place_ref[0]
    lanes = lax.broadcasted_iota(jnp.int32, counts_ref.shape, 1)
    count = jnp.sum(jnp.where(lanes == region, counts_ref[...], 0), axis=1, keepdims=True)
    sites = lax.broadcasted_iota(jnp.int32, (1, half), 1)
    for part, out in ((0, head_ref), (1, tail_ref)):
        row = pl.ds(2 * region + part, 1)
        mask = jnp.where(sites + part * half < count, 1.0, 0.0)
        root = jnp.sqrt(weights_ref[row, :] * mask)
        full = obs_ref[:, part * half : (part + 1) * half].astype(jnp.float32)
        centre = jnp.sum(full, axis=0, keepdims=True) * (1.0 / members)
        out[0:members, :] = ((full - centre) * root).astype(jnp.bfloat16)
        innov = root * (values_ref[row, :] - centre)
        out[members:, :] = jnp.broadcast_to(innov, (PAD, half)).astype(jnp.bfloat16)


def weights_kernel(left_ref, head_ref, tail_ref, right_ref, table_ref, out_ref, gains, turned):
    members, sites = gains.shape
    half = sites // 4
    parts = (left_ref, head_ref, tail_ref, right_ref)
    for part, ref in enumerate(parts):
        block = ref[0:members, :]
        gains[:, part * half : (part + 1) * half] = block
        turned[part * half : (part + 1) * half, :] = block.T
    innov = jnp.concatenate([ref[members:, :] for ref in parts], axis=1)

    normal = dot(turned[...], gains[...]) * (1.0 / (members - 1))
    upper = jnp.max(jnp.sum(jnp.abs(normal), axis=0, keepdims=True), axis=1, keepdims=True) + 1e-06
    nodes = upper * table_ref[NODES : NODES + 1, :]
    lifted = jnp.sqrt(1.0 + nodes)
    table = table_ref[0:NODES, :]
    roots = jnp.sum(table * (-1.0 / (lifted * (1.0 + lifted))), axis=1, keepdims=True)
    inverses = jnp.sum(table * (1.0 / (1.0 + nodes)), axis=1, keepdims=True)
    a = [roots[k : k + 1, :] for k in range(NODES)]
    e = [inverses[k : k + 1, :] for k in range(NODES)]

    rows = lax.broadcasted_iota(jnp.int32, normal.shape, 0)
    columns = lax.broadcasted_iota(jnp.int32, normal.shape, 1)
    eye = jnp.where(rows == columns, 1.0, 0.0).astype(jnp.float32)
    scaled = normal * (2.0 / upper)
    scaled_parts = split(scaled)
    t1 = scaled - eye
    t2 = 2.0 * product(scaled_parts, scaled_parts) - 4.0 * scaled + eye
    t2_parts = split(t2)
    t3 = 2.0 * (product(t2_parts, scaled_parts) - t2) - t1
    t4 = 2.0 * product(t2_parts, t2_parts) - eye
    t4_parts = split(t4)

    def polynomial(c):
        inner = c[5] * t1 + c[6] * t2 + c[7] * t3
        outer = c[0] * eye + (c[1] - c[7]) * t1 + (c[2] - c[6]) * t2 + (c[3] - c[5]) * t3 + c[4] * t4
        return outer + 2.0 * product(split(inner), t4_parts)

    root = split(polynomial(a))
    inverse = split(polynomial(e))
    mean_weights = dot(innov, inverse[0]) + dot(innov, inverse[1])
    shift = split(mean_weights * (1.0 / (members - 1)))
    turned_now = turned[...]
    rows_shift = dot(shift[0], turned_now) + dot(shift[1], turned_now)
    high, low = split(rows_shift[0:1, :])
    extra = lax.broadcasted_iota(jnp.int32, (PAD, members), 0)
    high, low = (jnp.broadcast_to(row.astype(jnp.float32), (PAD, members)) for row in (high, low))
    ones = jnp.where(extra == ONES, 1.0, 0.0)
    below = jnp.where(extra == HIGH, high, jnp.where(extra == LOW, low, ones))
    out_ref[members:, 0:members] = below.astype(jnp.bfloat16)
    reduced = (dot(root[0], turned_now) + dot(root[1], turned_now)).astype(jnp.bfloat16)
    out_ref[0:members, 0:members] = (dot(gains[...], reduced) * (1.0 / (members - 1))).astype(jnp.bfloat16)
    high, low = split(dot(out_ref[:, 0:members], jnp.ones((members, 128), jnp.bfloat16)))
    lanes = lax.broadcasted_iota(jnp.int32, high.shape, 1)
    high, low = high.astype(jnp.float32), low.astype(jnp.float32)
    sums = jnp.where(lanes < 2, high, jnp.where(lanes == 2, low, 0.0))
    out_ref[:, members:] = sums.astype(jnp.bfloat16)


def apply_kernel(state_ref, weights_ref, out_ref):
    members, columns = state_ref.shape
    state = state_ref[...]
    below = dot(weights_ref[members:, 0:members], state)
    high, low = split(below[ONES : ONES + 1, :] * (-1.0 / members))
    rows = lax.broadcasted_iota(jnp.int32, (128, columns), 0)
    high, low = high.astype(jnp.float32), low.astype(jnp.float32)
    centre = jnp.where(rows == 1, low, jnp.where(rows < 3, high, 0.0)).astype(jnp.bfloat16)
    below = below + dot(weights_ref[members:, members:], centre)
    shift = below[HIGH : HIGH + 1, :] + below[LOW : LOW + 1, :]
    step = 256
    for start in range(0, members, step):
        block = slice(start, start + step)
        update = dot(weights_ref[block, 0:members], state) + dot(weights_ref[block, members:], centre)
        out_ref[block, :] = (state_ref[block, :].astype(jnp.float32) + shift + update).astype(jnp.bfloat16)


def gather_kernel(array_ref, out_ref, done):
    count, _, width = out_ref.shape
    copies = [
        pltpu.make_async_copy(array_ref.at[:, pl.ds(k * width, width)], out_ref.at[k], done.at[k])
        for k in range(count)
    ]
    for copy in copies:
        copy.start()
    for copy in copies:
        copy.wait()


VMEM = pl.BlockSpec(memory_space=pltpu.VMEM)
SMEM = pl.BlockSpec(memory_space=pltpu.SMEM)
HBM = pl.BlockSpec(memory_space=pltpu.HBM)
ANY = pl.BlockSpec(memory_space=pl.ANY)


def struct(shape):
    return jax.ShapeDtypeStruct(shape[1:], shape[0])


def call(kernel, args, specs, outs, out_specs, scratch=(), flops=10**6, nbytes=10**6, mib=8):
    return pl.pallas_call(
        kernel,
        out_shape=jax.tree.map(struct, outs, is_leaf=lambda x: isinstance(x, tuple)),
        in_specs=specs,
        out_specs=out_specs,
        scratch_shapes=list(scratch),
        compiler_params=pltpu.CompilerParams(vmem_limit_bytes=mib * 1024 * 1024),
        cost_estimate=pl.CostEstimate(flops=flops, bytes_accessed=nbytes, transcendentals=0),
    )(*args)


def on_device(state, obs_ens, obs_values, obs_weight, counts):
    mem_index = lax.axis_index("mem").astype(jnp.int32).reshape(1)
    devices = lax.axis_size("mem")
    patches = lax.axis_size("patch")
    share = obs_ens.shape[0]
    own = obs_ens.shape[1] // devices
    half = own // 2
    bf16 = jnp.bfloat16

    blocks = call(
        gather_kernel, (pltpu.with_memory_space_constraint(obs_ens, pltpu.HBM),), [HBM], (bf16, devices, share, own), ANY,
        [pltpu.SemaphoreType.DMA((devices,))],
    )
    region_obs = lax.all_to_all(blocks, "mem", split_axis=0, concat_axis=0, tiled=True)
    region_obs = region_obs.reshape(devices * share, own)
    region_state = lax.all_to_all(state, "mem", split_axis=1, concat_axis=0, tiled=True)
    members, columns = region_state.shape

    edge = (bf16, members + PAD, half)
    head, tail = call(
        gains_kernel,
        (mem_index, region_obs, obs_values.reshape(-1, half), obs_weight.reshape(-1, half), counts.reshape(1, -1)),
        [SMEM, VMEM, VMEM, VMEM, VMEM], [edge, edge], [VMEM, VMEM],
    )
    left = lax.ppermute(tail, "patch", [(i, (i + 1) % patches) for i in range(patches)])
    right = lax.ppermute(head, "patch", [((i + 1) % patches, i) for i in range(patches)])
    transform = call(
        weights_kernel, (left, head, tail, right, jnp.asarray(tables())), [VMEM] * 5,
        (bf16, members + PAD, members + 128), VMEM,
        [pltpu.VMEM((members, 2 * own), bf16), pltpu.VMEM((2 * own, members), bf16)],
        7 * 10**9, 4 * 10**6, 24,
    )
    analysed = call(
        apply_kernel, (region_state, transform), [VMEM] * 2, (bf16, members, columns), VMEM,
        (), 10**9, 4 * 10**6, 8,
    )
    return lax.all_to_all(analysed, "mem", split_axis=0, concat_axis=1, tiled=True)


def solution(mesh):
    placed = (P("mem", "patch"), P("mem", "patch"), P("patch"), P("patch"), P("patch"))
    return jax.shard_map(
        on_device, mesh=mesh, in_specs=placed, out_specs=P("mem", "patch"), check_vma=False
    )
```

```python
import math

import jax
import jax.numpy as jnp
import numpy as np
from jax import lax
from jax.experimental import pallas as pl
from jax.experimental.pallas import tpu as pltpu
from jax.sharding import PartitionSpec as P

DEGREE = 7
NODES = DEGREE + 1
PAD = 16
HIGH, LOW, ONES = 0, 1, 2


def tables():
    theta = (np.arange(NODES) + 0.5) * (math.pi / NODES)
    orders = np.arange(NODES)
    table = np.zeros((2 * NODES, 128), np.float32)
    weight = np.where(orders == 0, 0.5, 1.0) * 2.0 / NODES
    table[:NODES, :NODES] = np.cos(orders[:, None] * theta[None, :]) * weight[:, None]
    table[NODES, :NODES] = (np.cos(theta) + 1.0) * 0.5
    return table


def dot(left, right):
    return jnp.dot(left, right, preferred_element_type=jnp.float32)


def split(x):
    high = x.astype(jnp.bfloat16)
    return high, (x - high.astype(jnp.float32)).astype(jnp.bfloat16)


def product(left, right):
    return dot(left[0], right[0]) + (dot(left[0], right[1]) + dot(left[1], right[0]))


def gains_kernel(place_ref, obs_ref, values_ref, weights_ref, counts_ref, head_ref, tail_ref):
    members, own = obs_ref.shape
    half = own // 2
    region = place_ref[0]
    lanes = lax.broadcasted_iota(jnp.int32, counts_ref.shape, 1)
    count = jnp.sum(jnp.where(lanes == region, counts_ref[...], 0), axis=1, keepdims=True)
    sites = lax.broadcasted_iota(jnp.int32, (1, half), 1)
    for part, out in ((0, head_ref), (1, tail_ref)):
        row = pl.ds(2 * region + part, 1)
        mask = jnp.where(sites + part * half < count, 1.0, 0.0)
        root = jnp.sqrt(weights_ref[row, :] * mask)
        full = obs_ref[:, part * half : (part + 1) * half].astype(jnp.float32)
        centre = jnp.sum(full, axis=0, keepdims=True) * (1.0 / members)
        out[0:members, :] = ((full - centre) * root).astype(jnp.bfloat16)
        innov = root * (values_ref[row, :] - centre)
        out[members:, :] = jnp.broadcast_to(innov, (PAD, half)).astype(jnp.bfloat16)


def weights_kernel(left_ref, head_ref, tail_ref, right_ref, table_ref, out_ref, gains, turned):
    members, sites = gains.shape
    half = sites // 4
    parts = (left_ref, head_ref, tail_ref, right_ref)
    for part, ref in enumerate(parts):
        block = ref[0:members, :]
        gains[:, part * half : (part + 1) * half] = block
        turned[part * half : (part + 1) * half, :] = block.T
    innov = jnp.concatenate([ref[members:, :] for ref in parts], axis=1)

    normal = dot(turned[...], gains[...]) * (1.0 / (members - 1))
    upper = jnp.max(jnp.sum(jnp.abs(normal), axis=0, keepdims=True), axis=1, keepdims=True) + 1e-06
    nodes = upper * table_ref[NODES : NODES + 1, :]
    lifted = jnp.sqrt(1.0 + nodes)
    table = table_ref[0:NODES, :]
    roots = jnp.sum(table * (-1.0 / (lifted * (1.0 + lifted))), axis=1, keepdims=True)
    inverses = jnp.sum(table * (1.0 / (1.0 + nodes)), axis=1, keepdims=True)
    a = [roots[k : k + 1, :] for k in range(NODES)]
    e = [inverses[k : k + 1, :] for k in range(NODES)]

    rows = lax.broadcasted_iota(jnp.int32, normal.shape, 0)
    columns = lax.broadcasted_iota(jnp.int32, normal.shape, 1)
    eye = jnp.where(rows == columns, 1.0, 0.0).astype(jnp.float32)
    scaled = normal * (2.0 / upper)
    scaled_parts = split(scaled)
    t1 = scaled - eye
    t2 = 2.0 * product(scaled_parts, scaled_parts) - 4.0 * scaled + eye
    t2_parts = split(t2)
    t3 = 2.0 * (product(t2_parts, scaled_parts) - t2) - t1
    t4 = 2.0 * product(t2_parts, t2_parts) - eye
    t4_parts = split(t4)

    def polynomial(c):
        inner = c[5] * t1 + c[6] * t2 + c[7] * t3
        outer = c[0] * eye + (c[1] - c[7]) * t1 + (c[2] - c[6]) * t2 + (c[3] - c[5]) * t3 + c[4] * t4
        return outer + 2.0 * product(split(inner), t4_parts)

    root = split(polynomial(a))
    inverse = split(polynomial(e))
    mean_weights = dot(innov, inverse[0]) + dot(innov, inverse[1])
    shift = split(mean_weights * (1.0 / (members - 1)))
    turned_now = turned[...]
    rows_shift = dot(shift[0], turned_now) + dot(shift[1], turned_now)
    high, low = split(rows_shift[0:1, :])
    extra = lax.broadcasted_iota(jnp.int32, (PAD, members), 0)
    high, low = (jnp.broadcast_to(row.astype(jnp.float32), (PAD, members)) for row in (high, low))
    ones = jnp.where(extra == ONES, 1.0, 0.0)
    below = jnp.where(extra == HIGH, high, jnp.where(extra == LOW, low, ones))
    out_ref[members:, 0:members] = below.astype(jnp.bfloat16)
    reduced = (dot(root[0], turned_now) + dot(root[1], turned_now)).astype(jnp.bfloat16)
    out_ref[0:members, 0:members] = (dot(gains[...], reduced) * (1.0 / (members - 1))).astype(jnp.bfloat16)
    high, low = split(dot(out_ref[:, 0:members], jnp.ones((members, 128), jnp.bfloat16)))
    lanes = lax.broadcasted_iota(jnp.int32, high.shape, 1)
    high, low = high.astype(jnp.float32), low.astype(jnp.float32)
    sums = jnp.where(lanes < 2, high, jnp.where(lanes == 2, low, 0.0))
    out_ref[:, members:] = sums.astype(jnp.bfloat16)


def apply_kernel(state_ref, weights_ref, out_ref):
    members, columns = state_ref.shape
    state = state_ref[...]
    below = dot(weights_ref[members:, 0:members], state)
    high, low = split(below[ONES : ONES + 1, :] * (-1.0 / members))
    rows = lax.broadcasted_iota(jnp.int32, (128, columns), 0)
    high, low = high.astype(jnp.float32), low.astype(jnp.float32)
    centre = jnp.where(rows == 1, low, jnp.where(rows < 3, high, 0.0)).astype(jnp.bfloat16)
    below = below + dot(weights_ref[members:, members:], centre)
    shift = below[HIGH : HIGH + 1, :] + below[LOW : LOW + 1, :]
    step = 256
    for start in range(0, members, step):
        block = slice(start, start + step)
        update = dot(weights_ref[block, 0:members], state) + dot(weights_ref[block, members:], centre)
        out_ref[block, :] = (state_ref[block, :].astype(jnp.float32) + shift + update).astype(jnp.bfloat16)


def gather_kernel(array_ref, out_ref, done):
    count, _, width = out_ref.shape
    copies = [
        pltpu.make_async_copy(array_ref.at[:, pl.ds(k * width, width)], out_ref.at[k], done.at[k])
        for k in range(count)
    ]
    for copy in copies:
        copy.start()
    for copy in copies:
        copy.wait()


VMEM = pl.BlockSpec(memory_space=pltpu.VMEM)
SMEM = pl.BlockSpec(memory_space=pltpu.SMEM)
ANY = pl.BlockSpec(memory_space=pl.ANY)


def struct(shape):
    return jax.ShapeDtypeStruct(shape[1:], shape[0])


def call(kernel, args, specs, outs, out_specs, scratch=(), flops=10**6, nbytes=10**6, mib=8):
    return pl.pallas_call(
        kernel,
        out_shape=jax.tree.map(struct, outs, is_leaf=lambda x: isinstance(x, tuple)),
        in_specs=specs,
        out_specs=out_specs,
        scratch_shapes=list(scratch),
        compiler_params=pltpu.CompilerParams(vmem_limit_bytes=mib * 1024 * 1024),
        cost_estimate=pl.CostEstimate(flops=flops, bytes_accessed=nbytes, transcendentals=0),
    )(*args)


def on_device(state, obs_ens, obs_values, obs_weight, counts):
    mem_index = lax.axis_index("mem").astype(jnp.int32).reshape(1)
    devices = lax.axis_size("mem")
    patches = lax.axis_size("patch")
    share = obs_ens.shape[0]
    own = obs_ens.shape[1] // devices
    half = own // 2
    bf16 = jnp.bfloat16

    blocks = call(
        gather_kernel, (obs_ens,), [VMEM], (bf16, devices, share, own), ANY,
        [pltpu.SemaphoreType.DMA((devices,))],
    )
    region_obs = lax.all_to_all(blocks, "mem", split_axis=0, concat_axis=0, tiled=True)
    region_obs = region_obs.reshape(devices * share, own)
    region_state = lax.all_to_all(state, "mem", split_axis=1, concat_axis=0, tiled=True)
    members, columns = region_state.shape

    edge = (bf16, members + PAD, half)
    head, tail = call(
        gains_kernel,
        (mem_index, region_obs, obs_values.reshape(-1, half), obs_weight.reshape(-1, half), counts.reshape(1, -1)),
        [SMEM, VMEM, VMEM, VMEM, VMEM], [edge, edge], [VMEM, VMEM],
    )
    left = lax.ppermute(tail, "patch", [(i, (i + 1) % patches) for i in range(patches)])
    right = lax.ppermute(head, "patch", [((i + 1) % patches, i) for i in range(patches)])
    transform = call(
        weights_kernel, (left, head, tail, right, jnp.asarray(tables())), [VMEM] * 5,
        (bf16, members + PAD, members + 128), VMEM,
        [pltpu.VMEM((members, 2 * own), bf16), pltpu.VMEM((2 * own, members), bf16)],
        7 * 10**9, 4 * 10**6, 24,
    )
    analysed = call(
        apply_kernel, (region_state, transform), [VMEM] * 2, (bf16, members, columns), VMEM,
        (), 10**9, 4 * 10**6, 8,
    )
    return lax.all_to_all(analysed, "mem", split_axis=0, concat_axis=1, tiled=True)


def solution(mesh):
    placed = (P("mem", "patch"), P("mem", "patch"), P("patch"), P("patch"), P("patch"))
    return jax.shard_map(
        on_device, mesh=mesh, in_specs=placed, out_specs=P("mem", "patch"), check_vma=False
    )
```

```python
import math

import jax
import jax.numpy as jnp
import numpy as np
from jax import lax
from jax.experimental import pallas as pl
from jax.experimental.pallas import tpu as pltpu
from jax.sharding import PartitionSpec as P

DEGREE = 7
NODES = DEGREE + 1
PAD = 16


def tables():
    theta = (np.arange(NODES) + 0.5) * (math.pi / NODES)
    orders = np.arange(NODES)
    table = np.zeros((2 * NODES, 128), np.float32)
    weight = np.where(orders == 0, 0.5, 1.0) * 2.0 / NODES
    table[:NODES, :NODES] = np.cos(orders[:, None] * theta[None, :]) * weight[:, None]
    table[NODES, :NODES] = (np.cos(theta) + 1.0) * 0.5
    return table


def dot(left, right):
    return jnp.dot(left, right, preferred_element_type=jnp.float32)


def split(x):
    high = x.astype(jnp.bfloat16)
    return high, (x - high.astype(jnp.float32)).astype(jnp.bfloat16)


def product(left, right):
    return dot(left[0], right[0]) + (dot(left[0], right[1]) + dot(left[1], right[0]))


def gains_kernel(place_ref, obs_ref, values_ref, weights_ref, counts_ref, head_ref, tail_ref):
    members, own = obs_ref.shape
    half = own // 2
    region = place_ref[0]
    lanes = lax.broadcasted_iota(jnp.int32, counts_ref.shape, 1)
    count = jnp.sum(jnp.where(lanes == region, counts_ref[...], 0), axis=1, keepdims=True)
    sites = lax.broadcasted_iota(jnp.int32, (1, half), 1)
    for part, out in ((0, head_ref), (1, tail_ref)):
        row = pl.ds(2 * region + part, 1)
        mask = jnp.where(sites + part * half < count, 1.0, 0.0)
        root = jnp.sqrt(weights_ref[row, :] * mask)
        full = obs_ref[:, part * half : (part + 1) * half].astype(jnp.float32)
        centre = jnp.sum(full, axis=0, keepdims=True) * (1.0 / members)
        out[0:members, :] = ((full - centre) * root).astype(jnp.bfloat16)
        innov = root * (values_ref[row, :] - centre)
        out[members:, :] = jnp.broadcast_to(innov, (PAD, half)).astype(jnp.bfloat16)


def weights_kernel(left_ref, head_ref, tail_ref, right_ref, table_ref, out_ref, gains, turned):
    members, sites = gains.shape
    half = sites // 4
    parts = (left_ref, head_ref, tail_ref, right_ref)
    for part, ref in enumerate(parts):
        block = ref[0:members, :]
        gains[:, part * half : (part + 1) * half] = block
        turned[part * half : (part + 1) * half, :] = block.T
    innov = jnp.concatenate([ref[members:, :] for ref in parts], axis=1)

    normal = dot(turned[...], gains[...]) * (1.0 / (members - 1))
    upper = jnp.max(jnp.sum(jnp.abs(normal), axis=0, keepdims=True), axis=1, keepdims=True) + 1e-06
    nodes = upper * table_ref[NODES : NODES + 1, :]
    lifted = jnp.sqrt(1.0 + nodes)
    table = table_ref[0:NODES, :]
    roots = jnp.sum(table * (-1.0 / (lifted * (1.0 + lifted))), axis=1, keepdims=True)
    inverses = jnp.sum(table * (1.0 / (1.0 + nodes)), axis=1, keepdims=True)
    a = [roots[k : k + 1, :] for k in range(NODES)]
    e = [inverses[k : k + 1, :] for k in range(NODES)]

    rows = lax.broadcasted_iota(jnp.int32, normal.shape, 0)
    columns = lax.broadcasted_iota(jnp.int32, normal.shape, 1)
    eye = jnp.where(rows == columns, 1.0, 0.0).astype(jnp.float32)
    scaled = normal * (2.0 / upper)
    scaled_parts = split(scaled)
    t1 = scaled - eye
    t2 = 2.0 * product(scaled_parts, scaled_parts) - 4.0 * scaled + eye
    t2_parts = split(t2)
    t3 = 2.0 * (product(t2_parts, scaled_parts) - t2) - t1
    t4 = 2.0 * product(t2_parts, t2_parts) - eye
    t4_parts = split(t4)

    def split_polynomial(c):
        inner = c[5] * t1 + c[6] * t2 + c[7] * t3
        outer = c[0] * eye + (c[1] - c[7]) * t1 + (c[2] - c[6]) * t2 + (c[3] - c[5]) * t3 + c[4] * t4
        return split(inner), outer

    inner, outer = split_polynomial(e)
    outer = split(outer)
    row = dot(innov, outer[0]) + dot(innov, outer[1])
    row = row + 2.0 * product(split(dot(innov, inner[0]) + dot(innov, inner[1])), t4_parts)
    shift = split(row * (1.0 / (members - 1)))
    across = turned[...]
    row = dot(shift[0], across) + dot(shift[1], across)
    row = row - jnp.sum(row, axis=1, keepdims=True) * (1.0 / members)
    high, low = (part.astype(jnp.float32) for part in split(row))
    below = jnp.where(lax.broadcasted_iota(jnp.int32, row.shape, 0) < PAD // 2, high, low)
    out_ref[members:, :] = below.astype(jnp.bfloat16)

    inner, outer = split_polynomial(a)
    root = split(outer + 2.0 * product(inner, t4_parts))
    reduced = dot(root[0], across) + dot(root[1], across)
    reduced = reduced - jnp.sum(reduced, axis=1, keepdims=True) * (1.0 / members)
    update = dot(gains[...], reduced.astype(jnp.bfloat16))
    out_ref[0:members, :] = (update * (1.0 / (members - 1))).astype(jnp.bfloat16)


def apply_kernel(state_ref, weights_ref, out_ref):
    members = state_ref.shape[0]
    below = dot(weights_ref[members:, :], state_ref[...])
    shift = below[0:1, :] + below[PAD // 2 : PAD // 2 + 1, :]
    step = 256
    for start in range(0, members, step):
        block = slice(start, start + step)
        update = dot(weights_ref[block, :], state_ref[...])
        out_ref[block, :] = (state_ref[block, :].astype(jnp.float32) + shift + update).astype(jnp.bfloat16)


def gather_kernel(array_ref, out_ref, done):
    count, _, width = out_ref.shape
    copies = [
        pltpu.make_async_copy(array_ref.at[:, pl.ds(k * width, width)], out_ref.at[k], done.at[k])
        for k in range(count)
    ]
    for copy in copies:
        copy.start()
    for copy in copies:
        copy.wait()


VMEM = pl.BlockSpec(memory_space=pltpu.VMEM)
SMEM = pl.BlockSpec(memory_space=pltpu.SMEM)
ANY = pl.BlockSpec(memory_space=pl.ANY)


def struct(shape):
    return jax.ShapeDtypeStruct(shape[1:], shape[0])


def call(kernel, args, specs, outs, out_specs, scratch=(), flops=10**6, nbytes=10**6, mib=8):
    return pl.pallas_call(
        kernel,
        out_shape=jax.tree.map(struct, outs, is_leaf=lambda x: isinstance(x, tuple)),
        in_specs=specs,
        out_specs=out_specs,
        scratch_shapes=list(scratch),
        compiler_params=pltpu.CompilerParams(vmem_limit_bytes=mib * 1024 * 1024),
        cost_estimate=pl.CostEstimate(flops=flops, bytes_accessed=nbytes, transcendentals=0),
    )(*args)


def on_device(state, obs_ens, obs_values, obs_weight, counts):
    mem_index = lax.axis_index("mem").astype(jnp.int32).reshape(1)
    devices = lax.axis_size("mem")
    patches = lax.axis_size("patch")
    share = obs_ens.shape[0]
    own = obs_ens.shape[1] // devices
    half = own // 2
    bf16 = jnp.bfloat16

    blocks = call(
        gather_kernel, (obs_ens,), [VMEM], (bf16, devices, share, own), ANY,
        [pltpu.SemaphoreType.DMA((devices,))],
    )
    region_obs = lax.all_to_all(blocks, "mem", split_axis=0, concat_axis=0, tiled=True)
    region_obs = region_obs.reshape(devices * share, own)
    region_state = lax.all_to_all(state, "mem", split_axis=1, concat_axis=0, tiled=True)
    members, columns = region_state.shape

    edge = (bf16, members + PAD, half)
    head, tail = call(
        gains_kernel,
        (mem_index, region_obs, obs_values.reshape(-1, half), obs_weight.reshape(-1, half), counts.reshape(1, -1)),
        [SMEM, VMEM, VMEM, VMEM, VMEM], [edge, edge], [VMEM, VMEM],
    )
    left = lax.ppermute(tail, "patch", [(i, (i + 1) % patches) for i in range(patches)])
    right = lax.ppermute(head, "patch", [((i + 1) % patches, i) for i in range(patches)])
    transform = call(
        weights_kernel, (left, head, tail, right, jnp.asarray(tables())), [VMEM] * 5,
        (bf16, members + PAD, members), VMEM,
        [pltpu.VMEM((members, 2 * own), bf16), pltpu.VMEM((2 * own, members), bf16)],
        7 * 10**9, 4 * 10**6, 24,
    )
    analysed = call(
        apply_kernel, (region_state, transform), [VMEM] * 2, (bf16, members, columns), VMEM,
        (), 10**9, 4 * 10**6, 8,
    )
    return lax.all_to_all(analysed, "mem", split_axis=0, concat_axis=1, tiled=True)


def solution(mesh):
    placed = (P("mem", "patch"), P("mem", "patch"), P("patch"), P("patch"), P("patch"))
    return jax.shard_map(
        on_device, mesh=mesh, in_specs=placed, out_specs=P("mem", "patch"), check_vma=False
    )
```

```python
import math

import jax
import jax.numpy as jnp
import numpy as np
from jax import lax
from jax.experimental import pallas as pl
from jax.experimental.pallas import tpu as pltpu
from jax.sharding import PartitionSpec as P

DEGREE = 7
NODES = DEGREE + 1
PAD = 16
GROUP = 8


def tables():
    theta = (np.arange(NODES) + 0.5) * (math.pi / NODES)
    orders = np.arange(NODES)
    table = np.zeros((2 * NODES, 128), np.float32)
    weight = np.where(orders == 0, 0.5, 1.0) * 2.0 / NODES
    table[:NODES, :NODES] = np.cos(orders[:, None] * theta[None, :]) * weight[:, None]
    table[NODES, :NODES] = (np.cos(theta) + 1.0) * 0.5
    return table


def dot(left, right):
    return jnp.dot(left, right, preferred_element_type=jnp.float32)


def split(x):
    high = x.astype(jnp.bfloat16)
    return high, (x - high.astype(jnp.float32)).astype(jnp.bfloat16)


def product(left, right):
    return dot(left[0], right[0]) + (dot(left[0], right[1]) + dot(left[1], right[0]))


def gains_kernel(place_ref, obs_ref, values_ref, weights_ref, counts_ref, head_ref, tail_ref):
    members, own = obs_ref.shape
    half = own // 2
    region = place_ref[0]
    lanes = lax.broadcasted_iota(jnp.int32, counts_ref.shape, 1)
    count = jnp.sum(jnp.where(lanes == region, counts_ref[...], 0), axis=1, keepdims=True)
    sites = lax.broadcasted_iota(jnp.int32, (1, half), 1)
    for part, out in ((0, head_ref), (1, tail_ref)):
        row = pl.ds(2 * region + part, 1)
        mask = jnp.where(sites + part * half < count, 1.0, 0.0)
        root = jnp.sqrt(weights_ref[row, :] * mask)
        full = obs_ref[:, part * half : (part + 1) * half].astype(jnp.float32)
        centre = jnp.sum(full, axis=0, keepdims=True) * (1.0 / members)
        out[0:members, :] = ((full - centre) * root).astype(jnp.bfloat16)
        innov = root * (values_ref[row, :] - centre)
        out[members:, :] = jnp.broadcast_to(innov, (PAD, half)).astype(jnp.bfloat16)


def weights_kernel(left_ref, head_ref, tail_ref, right_ref, table_ref, out_ref, gains, turned):
    members, sites = gains.shape
    half = sites // 4
    parts = (left_ref, head_ref, tail_ref, right_ref)
    for part, ref in enumerate(parts):
        block = ref[0:members, :]
        gains[:, part * half : (part + 1) * half] = block
        turned[part * half : (part + 1) * half, :] = block.T
    innov = jnp.concatenate([ref[members:, :] for ref in parts], axis=1)

    normal = dot(turned[...], gains[...]) * (1.0 / (members - 1))
    upper = jnp.max(jnp.sum(jnp.abs(normal), axis=0, keepdims=True), axis=1, keepdims=True) + 1e-06
    nodes = upper * table_ref[NODES : NODES + 1, :]
    lifted = jnp.sqrt(1.0 + nodes)
    table = table_ref[0:NODES, :]
    roots = jnp.sum(table * (-1.0 / (lifted * (1.0 + lifted))), axis=1, keepdims=True)
    inverses = jnp.sum(table * (1.0 / (1.0 + nodes)), axis=1, keepdims=True)
    a = [roots[k : k + 1, :] for k in range(NODES)]
    e = [inverses[k : k + 1, :] for k in range(NODES)]

    rows = lax.broadcasted_iota(jnp.int32, normal.shape, 0)
    columns = lax.broadcasted_iota(jnp.int32, normal.shape, 1)
    eye = jnp.where(rows == columns, 1.0, 0.0).astype(jnp.float32)
    scaled = normal * (2.0 / upper)
    scaled_parts = split(scaled)
    t1 = scaled - eye
    t2 = 2.0 * product(scaled_parts, scaled_parts) - 4.0 * scaled + eye
    t2_parts = split(t2)
    t3 = 2.0 * (product(t2_parts, scaled_parts) - t2) - t1
    t4 = 2.0 * product(t2_parts, t2_parts) - eye
    t4_parts = split(t4)

    def split_polynomial(c):
        inner = c[5] * t1 + c[6] * t2 + c[7] * t3
        outer = c[0] * eye + (c[1] - c[7]) * t1 + (c[2] - c[6]) * t2 + (c[3] - c[5]) * t3 + c[4] * t4
        return split(inner), outer

    inner, outer = split_polynomial(e)
    outer = split(outer)
    row = dot(innov, outer[0]) + dot(innov, outer[1])
    row = row + 2.0 * product(split(dot(innov, inner[0]) + dot(innov, inner[1])), t4_parts)
    shift = split(row * (1.0 / (members - 1)))
    across = turned[...]
    row = dot(shift[0], across) + dot(shift[1], across)
    row = row - jnp.sum(row, axis=1, keepdims=True) * (1.0 / members)
    high, low = (part.astype(jnp.float32) for part in split(row))
    below = jnp.where(lax.broadcasted_iota(jnp.int32, row.shape, 0) < PAD // 2, high, low)
    out_ref[members:, :] = below.astype(jnp.bfloat16)

    inner, outer = split_polynomial(a)
    root = split(outer + 2.0 * product(inner, t4_parts))
    reduced = dot(root[0], across) + dot(root[1], across)
    reduced = reduced - jnp.sum(reduced, axis=1, keepdims=True) * (1.0 / members)
    update = dot(gains[...], reduced.astype(jnp.bfloat16))
    out_ref[0:members, :] = (update * (1.0 / (members - 1))).astype(jnp.bfloat16)


def apply_kernel(state_ref, weights_ref, out_ref):
    members = state_ref.shape[0]
    below = dot(weights_ref[members:, :], state_ref[...])
    shift = below[0:1, :] + below[PAD // 2 : PAD // 2 + 1, :]
    step = 256
    for start in range(0, members, step):
        block = slice(start, start + step)
        update = dot(weights_ref[block, :], state_ref[...])
        out_ref[block, :] = (state_ref[block, :].astype(jnp.float32) + shift + update).astype(jnp.bfloat16)


def gather_kernel(array_ref, out_ref, held, came, left):
    count = array_ref.shape[0]
    inward = [pltpu.make_async_copy(array_ref.at[k], held.at[k], came.at[k]) for k in range(count)]
    outward = [pltpu.make_async_copy(held.at[k], out_ref.at[:, k], left.at[k]) for k in range(count)]
    for copy in inward:
        copy.start()
    for arrived, copy in zip(inward, outward):
        arrived.wait()
        copy.start()
    for copy in outward:
        copy.wait()


VMEM = pl.BlockSpec(memory_space=pltpu.VMEM)
SMEM = pl.BlockSpec(memory_space=pltpu.SMEM)
HBM = pl.BlockSpec(memory_space=pltpu.HBM)


def struct(shape):
    return jax.ShapeDtypeStruct(shape[1:], shape[0])


def call(kernel, args, specs, outs, out_specs, scratch=(), flops=10**6, nbytes=10**6, mib=8):
    return pl.pallas_call(
        kernel,
        out_shape=jax.tree.map(struct, outs, is_leaf=lambda x: isinstance(x, tuple)),
        in_specs=specs,
        out_specs=out_specs,
        scratch_shapes=list(scratch),
        compiler_params=pltpu.CompilerParams(vmem_limit_bytes=mib * 1024 * 1024),
        cost_estimate=pl.CostEstimate(flops=flops, bytes_accessed=nbytes, transcendentals=0),
    )(*args)


def on_device(state, obs_ens, obs_values, obs_weight, counts):
    mem_index = lax.axis_index("mem").astype(jnp.int32).reshape(1)
    devices = lax.axis_size("mem")
    patches = lax.axis_size("patch")
    share = obs_ens.shape[0]
    own = obs_ens.shape[1] // devices
    half = own // 2
    bf16 = jnp.bfloat16

    groups = share // GROUP

    def exchanged(array):
        width = array.shape[1] // devices
        tiles = array.reshape(groups, GROUP, devices, width).transpose(0, 2, 1, 3)
        blocks = call(
            gather_kernel, (pltpu.with_memory_space_constraint(tiles, pltpu.HBM),), [HBM],
            (bf16, devices, groups, GROUP, width), HBM,
            [pltpu.VMEM(tiles.shape, bf16), pltpu.SemaphoreType.DMA((groups,)), pltpu.SemaphoreType.DMA((groups,))],
        )
        arrived = lax.all_to_all(blocks, "mem", split_axis=0, concat_axis=0, tiled=True)
        return arrived.reshape(devices * share, width)

    region_obs = exchanged(obs_ens)
    region_state = exchanged(state)
    members, columns = region_state.shape

    edge = (bf16, members + PAD, half)
    head, tail = call(
        gains_kernel,
        (mem_index, region_obs, obs_values.reshape(-1, half), obs_weight.reshape(-1, half), counts.reshape(1, -1)),
        [SMEM, VMEM, VMEM, VMEM, VMEM], [edge, edge], [VMEM, VMEM],
    )
    left = lax.ppermute(tail, "patch", [(i, (i + 1) % patches) for i in range(patches)])
    right = lax.ppermute(head, "patch", [((i + 1) % patches, i) for i in range(patches)])
    transform = call(
        weights_kernel, (left, head, tail, right, jnp.asarray(tables())), [VMEM] * 5,
        (bf16, members + PAD, members), VMEM,
        [pltpu.VMEM((members, 2 * own), bf16), pltpu.VMEM((2 * own, members), bf16)],
        7 * 10**9, 4 * 10**6, 24,
    )
    analysed = call(
        apply_kernel, (region_state, transform), [VMEM] * 2, (bf16, members, columns), VMEM,
        (), 10**9, 4 * 10**6, 8,
    )
    return lax.all_to_all(analysed, "mem", split_axis=0, concat_axis=1, tiled=True)


def solution(mesh):
    placed = (P("mem", "patch"), P("mem", "patch"), P("patch"), P("patch"), P("patch"))
    return jax.shard_map(
        on_device, mesh=mesh, in_specs=placed, out_specs=P("mem", "patch"), check_vma=False
    )
```

```python
import math

import jax
import jax.numpy as jnp
import numpy as np
from jax import lax
from jax.experimental import pallas as pl
from jax.experimental.pallas import tpu as pltpu
from jax.sharding import PartitionSpec as P

DEGREE = 7
NODES = DEGREE + 1
PAD = 16
GROUP = 8


def tables():
    theta = (np.arange(NODES) + 0.5) * (math.pi / NODES)
    orders = np.arange(NODES)
    table = np.zeros((2 * NODES, 128), np.float32)
    weight = np.where(orders == 0, 0.5, 1.0) * 2.0 / NODES
    table[:NODES, :NODES] = np.cos(orders[:, None] * theta[None, :]) * weight[:, None]
    table[NODES, :NODES] = (np.cos(theta) + 1.0) * 0.5
    return table


def dot(left, right):
    return jnp.dot(left, right, preferred_element_type=jnp.float32)


def split(x):
    high = x.astype(jnp.bfloat16)
    return high, (x - high.astype(jnp.float32)).astype(jnp.bfloat16)


def product(left, right):
    return dot(left[0], right[0]) + (dot(left[0], right[1]) + dot(left[1], right[0]))


def gains_kernel(place_ref, obs_ref, values_ref, weights_ref, counts_ref, head_ref, tail_ref):
    members, own = obs_ref.shape
    half = own // 2
    region = place_ref[0]
    lanes = lax.broadcasted_iota(jnp.int32, counts_ref.shape, 1)
    count = jnp.sum(jnp.where(lanes == region, counts_ref[...], 0), axis=1, keepdims=True)
    sites = lax.broadcasted_iota(jnp.int32, (1, half), 1)
    for part, out in ((0, head_ref), (1, tail_ref)):
        row = pl.ds(2 * region + part, 1)
        mask = jnp.where(sites + part * half < count, 1.0, 0.0)
        root = jnp.sqrt(weights_ref[row, :] * mask)
        full = obs_ref[:, part * half : (part + 1) * half].astype(jnp.float32)
        centre = jnp.sum(full, axis=0, keepdims=True) * (1.0 / members)
        out[0:members, :] = ((full - centre) * root).astype(jnp.bfloat16)
        innov = root * (values_ref[row, :] - centre)
        out[members:, :] = jnp.broadcast_to(innov, (PAD, half)).astype(jnp.bfloat16)


def own_kernel(head_ref, tail_ref, gains_ref, turned_ref, inner_ref):
    members, own = gains_ref.shape
    half = own // 2
    for part, ref in enumerate((head_ref, tail_ref)):
        block = ref[0:members, :]
        gains_ref[:, part * half : (part + 1) * half] = block
        turned_ref[part * half : (part + 1) * half, :] = block.T
    inner_ref[...] = dot(turned_ref[...], gains_ref[...])


def weights_kernel(
    left_ref, head_ref, tail_ref, right_ref, table_ref, own_ref, own_turned_ref, inner_ref, out_ref, gains, turned
):
    members, sites = gains.shape
    half = sites // 4
    own = 2 * half
    parts = (head_ref, tail_ref, left_ref, right_ref)
    gains[:, :own] = own_ref[...]
    turned[:own, :] = own_turned_ref[...]
    for part, ref in ((2, left_ref), (3, right_ref)):
        block = ref[0:members, :]
        gains[:, part * half : (part + 1) * half] = block
        turned[part * half : (part + 1) * half, :] = block.T
    innov = jnp.concatenate([ref[members:, :] for ref in parts], axis=1)

    inner = inner_ref[...]
    edge = dot(turned[own:, :], gains[...])
    cross = edge[:, :own]
    normal = jnp.concatenate([jnp.concatenate([inner, cross.T], axis=1), edge], axis=0) * (1.0 / (members - 1))
    upper = jnp.max(jnp.sum(jnp.abs(normal), axis=0, keepdims=True), axis=1, keepdims=True) + 1e-06
    nodes = upper * table_ref[NODES : NODES + 1, :]
    lifted = jnp.sqrt(1.0 + nodes)
    table = table_ref[0:NODES, :]
    roots = jnp.sum(table * (-1.0 / (lifted * (1.0 + lifted))), axis=1, keepdims=True)
    inverses = jnp.sum(table * (1.0 / (1.0 + nodes)), axis=1, keepdims=True)
    a = [roots[k : k + 1, :] for k in range(NODES)]
    e = [inverses[k : k + 1, :] for k in range(NODES)]

    rows = lax.broadcasted_iota(jnp.int32, normal.shape, 0)
    columns = lax.broadcasted_iota(jnp.int32, normal.shape, 1)
    eye = jnp.where(rows == columns, 1.0, 0.0).astype(jnp.float32)
    scaled = normal * (2.0 / upper)
    scaled_parts = split(scaled)
    t1 = scaled - eye
    t2 = 2.0 * product(scaled_parts, scaled_parts) - 4.0 * scaled + eye
    t2_parts = split(t2)
    t3 = 2.0 * (product(t2_parts, scaled_parts) - t2) - t1
    t4 = 2.0 * product(t2_parts, t2_parts) - eye
    t4_parts = split(t4)

    def split_polynomial(c):
        inner = c[5] * t1 + c[6] * t2 + c[7] * t3
        outer = c[0] * eye + (c[1] - c[7]) * t1 + (c[2] - c[6]) * t2 + (c[3] - c[5]) * t3 + c[4] * t4
        return split(inner), outer

    inner, outer = split_polynomial(e)
    outer = split(outer)
    row = dot(innov, outer[0]) + dot(innov, outer[1])
    row = row + 2.0 * product(split(dot(innov, inner[0]) + dot(innov, inner[1])), t4_parts)
    shift = split(row * (1.0 / (members - 1)))
    across = turned[...]
    row = dot(shift[0], across) + dot(shift[1], across)
    row = row - jnp.sum(row, axis=1, keepdims=True) * (1.0 / members)
    high, low = (part.astype(jnp.float32) for part in split(row))
    below = jnp.where(lax.broadcasted_iota(jnp.int32, row.shape, 0) < PAD // 2, high, low)
    out_ref[members:, :] = below.astype(jnp.bfloat16)

    inner, outer = split_polynomial(a)
    root = split(outer + 2.0 * product(inner, t4_parts))
    reduced = dot(root[0], across) + dot(root[1], across)
    reduced = reduced - jnp.sum(reduced, axis=1, keepdims=True) * (1.0 / members)
    update = dot(gains[...], reduced.astype(jnp.bfloat16))
    out_ref[0:members, :] = (update * (1.0 / (members - 1))).astype(jnp.bfloat16)


def apply_kernel(state_ref, weights_ref, out_ref):
    members = state_ref.shape[0]
    last = members - 128
    below = dot(weights_ref[last:, :], state_ref[...])
    update, below = below[: members - last, :], below[members - last :, :]
    shift = below[0:1, :] + below[PAD // 2 : PAD // 2 + 1, :]
    out_ref[last:members, :] = (state_ref[last:members, :].astype(jnp.float32) + shift + update).astype(jnp.bfloat16)
    update = dot(weights_ref[:last, :], state_ref[...])
    out_ref[:last, :] = (state_ref[:last, :].astype(jnp.float32) + shift + update).astype(jnp.bfloat16)


def gather_kernel(array_ref, out_ref, held, came, left):
    count = array_ref.shape[0]
    inward = [pltpu.make_async_copy(array_ref.at[k], held.at[k], came.at[k]) for k in range(count)]
    outward = [pltpu.make_async_copy(held.at[k], out_ref.at[:, k], left.at[k]) for k in range(count)]
    for copy in inward:
        copy.start()
    for arrived, copy in zip(inward, outward):
        arrived.wait()
        copy.start()
    for copy in outward:
        copy.wait()


VMEM = pl.BlockSpec(memory_space=pltpu.VMEM)
SMEM = pl.BlockSpec(memory_space=pltpu.SMEM)
HBM = pl.BlockSpec(memory_space=pltpu.HBM)


def struct(shape):
    return jax.ShapeDtypeStruct(shape[1:], shape[0])


def call(kernel, args, specs, outs, out_specs, scratch=(), flops=10**6, nbytes=10**6, mib=8):
    return pl.pallas_call(
        kernel,
        out_shape=jax.tree.map(struct, outs, is_leaf=lambda x: isinstance(x, tuple)),
        in_specs=specs,
        out_specs=out_specs,
        scratch_shapes=list(scratch),
        compiler_params=pltpu.CompilerParams(vmem_limit_bytes=mib * 1024 * 1024),
        cost_estimate=pl.CostEstimate(flops=flops, bytes_accessed=nbytes, transcendentals=0),
    )(*args)


def on_device(state, obs_ens, obs_values, obs_weight, counts):
    mem_index = lax.axis_index("mem").astype(jnp.int32).reshape(1)
    devices = lax.axis_size("mem")
    patches = lax.axis_size("patch")
    share = obs_ens.shape[0]
    own = obs_ens.shape[1] // devices
    half = own // 2
    bf16 = jnp.bfloat16

    groups = share // GROUP

    def exchanged(array):
        width = array.shape[1] // devices
        tiles = array.reshape(groups, GROUP, devices, width).transpose(0, 2, 1, 3)
        blocks = call(
            gather_kernel, (pltpu.with_memory_space_constraint(tiles, pltpu.HBM),), [HBM],
            (bf16, devices, groups, GROUP, width), HBM,
            [pltpu.VMEM(tiles.shape, bf16), pltpu.SemaphoreType.DMA((groups,)), pltpu.SemaphoreType.DMA((groups,))],
        )
        arrived = lax.all_to_all(blocks, "mem", split_axis=0, concat_axis=0, tiled=True)
        return arrived.reshape(devices * share, width)

    region_obs = exchanged(obs_ens)
    region_state = exchanged(state)
    members, columns = region_state.shape

    edge = (bf16, members + PAD, half)
    head, tail = call(
        gains_kernel,
        (mem_index, region_obs, obs_values.reshape(-1, half), obs_weight.reshape(-1, half), counts.reshape(1, -1)),
        [SMEM, VMEM, VMEM, VMEM, VMEM], [edge, edge], [VMEM, VMEM],
    )
    left = lax.ppermute(tail, "patch", [(i, (i + 1) % patches) for i in range(patches)])
    right = lax.ppermute(head, "patch", [((i + 1) % patches, i) for i in range(patches)])
    own_parts = call(
        own_kernel, (head, tail), [VMEM] * 2,
        [(bf16, members, own), (bf16, own, members), (jnp.float32, own, own)], [VMEM] * 3,
    )
    transform = call(
        weights_kernel, (left, head, tail, right, jnp.asarray(tables()), *own_parts), [VMEM] * 8,
        (bf16, members + PAD, members), VMEM,
        [pltpu.VMEM((members, 2 * own), bf16), pltpu.VMEM((2 * own, members), bf16)],
        7 * 10**9, 4 * 10**6, 24,
    )
    analysed = call(
        apply_kernel, (region_state, transform), [VMEM] * 2, (bf16, members, columns), VMEM,
        (), 10**9, 4 * 10**6, 8,
    )
    return lax.all_to_all(analysed, "mem", split_axis=0, concat_axis=1, tiled=True)


def solution(mesh):
    placed = (P("mem", "patch"), P("mem", "patch"), P("patch"), P("patch"), P("patch"))
    return jax.shard_map(
        on_device, mesh=mesh, in_specs=placed, out_specs=P("mem", "patch"), check_vma=False
    )
```

```python
import math

import jax
import jax.numpy as jnp
import numpy as np
from jax import lax
from jax.experimental import pallas as pl
from jax.experimental.pallas import tpu as pltpu
from jax.sharding import PartitionSpec as P

DEGREE = 7
NODES = DEGREE + 1
PAD = 16
GROUP = 8


def tables():
    theta = (np.arange(NODES) + 0.5) * (math.pi / NODES)
    orders = np.arange(NODES)
    table = np.zeros((2 * NODES, 128), np.float32)
    weight = np.where(orders == 0, 0.5, 1.0) * 2.0 / NODES
    table[:NODES, :NODES] = np.cos(orders[:, None] * theta[None, :]) * weight[:, None]
    table[NODES, :NODES] = (np.cos(theta) + 1.0) * 0.5
    return table


def dot(left, right):
    return jnp.dot(left, right, preferred_element_type=jnp.float32)


def split(x):
    high = x.astype(jnp.bfloat16)
    return high, (x - high.astype(jnp.float32)).astype(jnp.bfloat16)


def product(left, right):
    return dot(left[0], right[0]) + (dot(left[0], right[1]) + dot(left[1], right[0]))


def gains_kernel(place_ref, obs_ref, values_ref, weights_ref, counts_ref, head_ref, tail_ref):
    members, own = obs_ref.shape
    half = own // 2
    region = place_ref[0]
    lanes = lax.broadcasted_iota(jnp.int32, counts_ref.shape, 1)
    count = jnp.sum(jnp.where(lanes == region, counts_ref[...], 0), axis=1, keepdims=True)
    sites = lax.broadcasted_iota(jnp.int32, (1, half), 1)
    for part, out in ((0, head_ref), (1, tail_ref)):
        row = pl.ds(2 * region + part, 1)
        mask = jnp.where(sites + part * half < count, 1.0, 0.0)
        root = jnp.sqrt(weights_ref[row, :] * mask)
        full = obs_ref[:, part * half : (part + 1) * half].astype(jnp.float32)
        centre = jnp.sum(full, axis=0, keepdims=True) * (1.0 / members)
        out[0:members, :] = ((full - centre) * root).astype(jnp.bfloat16)
        innov = root * (values_ref[row, :] - centre)
        out[members:, :] = jnp.broadcast_to(innov, (PAD, half)).astype(jnp.bfloat16)


def own_kernel(head_ref, tail_ref, gains_ref, turned_ref, inner_ref):
    members, own = gains_ref.shape
    half = own // 2
    for part, ref in enumerate((head_ref, tail_ref)):
        block = ref[0:members, :]
        gains_ref[:, part * half : (part + 1) * half] = block
        turned_ref[part * half : (part + 1) * half, :] = block.T
    inner_ref[...] = dot(turned_ref[...], gains_ref[...])


def weights_kernel(
    left_ref, head_ref, tail_ref, right_ref, table_ref, own_ref, own_turned_ref, inner_ref, out_ref, gains, turned
):
    members, sites = gains.shape
    half = sites // 4
    own = 2 * half
    parts = (head_ref, tail_ref, left_ref, right_ref)
    gains[:, :own] = own_ref[...]
    turned[:own, :] = own_turned_ref[...]
    for part, ref in ((2, left_ref), (3, right_ref)):
        block = ref[0:members, :]
        gains[:, part * half : (part + 1) * half] = block
        turned[part * half : (part + 1) * half, :] = block.T
    innov = jnp.concatenate([ref[members:, :] for ref in parts], axis=1)

    inner = inner_ref[...]
    edge = dot(turned[own:, :], gains[...])
    cross = edge[:, :own]
    normal = jnp.concatenate([jnp.concatenate([inner, cross.T], axis=1), edge], axis=0) * (1.0 / (members - 1))
    upper = jnp.max(jnp.sum(jnp.abs(normal), axis=0, keepdims=True), axis=1, keepdims=True) + 1e-06
    nodes = upper * table_ref[NODES : NODES + 1, :]
    lifted = jnp.sqrt(1.0 + nodes)
    table = table_ref[0:NODES, :]
    roots = jnp.sum(table * (-1.0 / (lifted * (1.0 + lifted))), axis=1, keepdims=True)
    inverses = jnp.sum(table * (1.0 / (1.0 + nodes)), axis=1, keepdims=True)
    a = [roots[k : k + 1, :] for k in range(NODES)]
    e = [inverses[k : k + 1, :] for k in range(NODES)]

    rows = lax.broadcasted_iota(jnp.int32, normal.shape, 0)
    columns = lax.broadcasted_iota(jnp.int32, normal.shape, 1)
    eye = jnp.where(rows == columns, 1.0, 0.0).astype(jnp.float32)
    scaled = normal * (2.0 / upper)
    scaled_parts = split(scaled)
    t1 = scaled - eye
    t2 = 2.0 * product(scaled_parts, scaled_parts) - 4.0 * scaled + eye
    t2_parts = split(t2)
    t3 = 2.0 * (product(t2_parts, scaled_parts) - t2) - t1
    t4 = 2.0 * product(t2_parts, t2_parts) - eye
    t4_parts = split(t4)

    def split_polynomial(c):
        inner = c[5] * t1 + c[6] * t2 + c[7] * t3
        outer = c[0] * eye + (c[1] - c[7]) * t1 + (c[2] - c[6]) * t2 + (c[3] - c[5]) * t3 + c[4] * t4
        return split(inner), outer

    inner, outer = split_polynomial(e)
    outer = split(outer)
    row = dot(innov, outer[0]) + dot(innov, outer[1])
    row = row + 2.0 * product(split(dot(innov, inner[0]) + dot(innov, inner[1])), t4_parts)
    shift = split(row * (1.0 / (members - 1)))
    across = turned[...]
    row = dot(shift[0], across) + dot(shift[1], across)
    row = row - jnp.sum(row, axis=1, keepdims=True) * (1.0 / members)
    high, low = (part.astype(jnp.float32) for part in split(row))
    below = jnp.where(lax.broadcasted_iota(jnp.int32, row.shape, 0) < PAD // 2, high, low)
    out_ref[members:, :] = below.astype(jnp.bfloat16)

    inner, outer = split_polynomial(a)
    root = split(outer + 2.0 * product(inner, t4_parts))
    reduced = dot(root[0], across) + dot(root[1], across)
    reduced = reduced - jnp.sum(reduced, axis=1, keepdims=True) * (1.0 / members)
    update = dot(gains[...], reduced.astype(jnp.bfloat16))
    out_ref[0:members, :] = (update * (1.0 / (members - 1))).astype(jnp.bfloat16)


def apply_kernel(state_ref, weights_ref, out_ref):
    members = state_ref.shape[0]
    last = members - 128
    below = dot(weights_ref[last:, :], state_ref[...])
    update, below = below[: members - last, :], below[members - last :, :]
    shift = below[0:1, :] + below[PAD // 2 : PAD // 2 + 1, :]
    out_ref[last:members, :] = (state_ref[last:members, :].astype(jnp.float32) + shift + update).astype(jnp.bfloat16)
    update = dot(weights_ref[:last, :], state_ref[...])
    out_ref[:last, :] = (state_ref[:last, :].astype(jnp.float32) + shift + update).astype(jnp.bfloat16)


def gather_kernel(array_ref, out_ref, held, came, left):
    count = array_ref.shape[0]
    inward = [pltpu.make_async_copy(array_ref.at[k], held.at[k], came.at[k]) for k in range(count)]
    outward = [pltpu.make_async_copy(held.at[k], out_ref.at[:, k], left.at[k]) for k in range(count)]
    for copy in inward:
        copy.start()
    for arrived, copy in zip(inward, outward):
        arrived.wait()
        copy.start()
    for copy in outward:
        copy.wait()


def scatter_kernel(blocks_ref, out_ref, done):
    count, half = out_ref.shape[0], out_ref.shape[1] // 2
    copies = [
        pltpu.make_async_copy(
            blocks_ref.at[pl.ds(part * half, half), k], out_ref.at[k, pl.ds(part * half, half)], done.at[2 * k + part]
        )
        for k in range(count)
        for part in range(2)
    ]
    for copy in copies:
        copy.start()
    for copy in copies:
        copy.wait()


VMEM = pl.BlockSpec(memory_space=pltpu.VMEM)
SMEM = pl.BlockSpec(memory_space=pltpu.SMEM)
HBM = pl.BlockSpec(memory_space=pltpu.HBM)


def struct(shape):
    return jax.ShapeDtypeStruct(shape[1:], shape[0])


def call(kernel, args, specs, outs, out_specs, scratch=(), flops=10**6, nbytes=10**6, mib=8):
    return pl.pallas_call(
        kernel,
        out_shape=jax.tree.map(struct, outs, is_leaf=lambda x: isinstance(x, tuple)),
        in_specs=specs,
        out_specs=out_specs,
        scratch_shapes=list(scratch),
        compiler_params=pltpu.CompilerParams(vmem_limit_bytes=mib * 1024 * 1024),
        cost_estimate=pl.CostEstimate(flops=flops, bytes_accessed=nbytes, transcendentals=0),
    )(*args)


def on_device(state, obs_ens, obs_values, obs_weight, counts):
    mem_index = lax.axis_index("mem").astype(jnp.int32).reshape(1)
    devices = lax.axis_size("mem")
    patches = lax.axis_size("patch")
    share = obs_ens.shape[0]
    own = obs_ens.shape[1] // devices
    half = own // 2
    bf16 = jnp.bfloat16

    groups = share // GROUP

    def exchanged(array):
        width = array.shape[1] // devices
        tiles = array.reshape(groups, GROUP, devices, width).transpose(0, 2, 1, 3)
        blocks = call(
            gather_kernel, (pltpu.with_memory_space_constraint(tiles, pltpu.HBM),), [HBM],
            (bf16, devices, groups, GROUP, width), HBM,
            [pltpu.VMEM(tiles.shape, bf16), pltpu.SemaphoreType.DMA((groups,)), pltpu.SemaphoreType.DMA((groups,))],
        )
        arrived = lax.all_to_all(blocks, "mem", split_axis=0, concat_axis=0, tiled=True)
        return arrived.reshape(devices * share, width)

    region_obs = exchanged(obs_ens)
    region_state = exchanged(state)
    members, columns = region_state.shape

    edge = (bf16, members + PAD, half)
    head, tail = call(
        gains_kernel,
        (mem_index, region_obs, obs_values.reshape(-1, half), obs_weight.reshape(-1, half), counts.reshape(1, -1)),
        [SMEM, VMEM, VMEM, VMEM, VMEM], [edge, edge], [VMEM, VMEM],
    )
    left = lax.ppermute(tail, "patch", [(i, (i + 1) % patches) for i in range(patches)])
    right = lax.ppermute(head, "patch", [((i + 1) % patches, i) for i in range(patches)])
    own_parts = call(
        own_kernel, (head, tail), [VMEM] * 2,
        [(bf16, members, own), (bf16, own, members), (jnp.float32, own, own)], [VMEM] * 3,
    )
    transform = call(
        weights_kernel, (left, head, tail, right, jnp.asarray(tables()), *own_parts), [VMEM] * 8,
        (bf16, members + PAD, members), VMEM,
        [pltpu.VMEM((members, 2 * own), bf16), pltpu.VMEM((2 * own, members), bf16)],
        7 * 10**9, 4 * 10**6, 24,
    )
    analysed = call(
        apply_kernel, (region_state, transform), [VMEM] * 2, (bf16, members, columns), VMEM,
        (), 10**9, 4 * 10**6, 8,
    )
    returned = lax.all_to_all(
        analysed.reshape(devices, groups, GROUP, columns), "mem", split_axis=0, concat_axis=0, tiled=True
    )
    tiles = call(
        scatter_kernel, (returned,), [VMEM], (bf16, groups, devices, GROUP, columns), HBM,
        [pltpu.SemaphoreType.DMA((2 * groups,))],
    )
    return tiles.transpose(0, 2, 1, 3).reshape(share, devices * columns)


def solution(mesh):
    placed = (P("mem", "patch"), P("mem", "patch"), P("patch"), P("patch"), P("patch"))
    return jax.shard_map(
        on_device, mesh=mesh, in_specs=placed, out_specs=P("mem", "patch"), check_vma=False
    )
```
